32 devices in a mesh: dp: 16 (over z, y, core), ctx: 2 (over x).
Axes of the slice: x: 2, y: 2, z: 4, core: 2. Of those that a mesh axis runs over, the one named last changes fastest.
Arguments:
- tokens: bfloat16 [48, 1024, 768], P('dp', 'ctx'), may hold values from -6 to 6
- segments: int32 [48, 1024], P('dp'), may hold values from 0 to 3, as said below
- qkv_weight: bfloat16 [768, 2304], P(('dp', 'ctx')), may hold values from -0.21875 to 0.21875
- out_weight: bfloat16 [768, 768], P(('dp', 'ctx')), may hold values from -1.75 to 1.75
- up_weight: bfloat16 [768, 3072], P(('dp', 'ctx')), may hold values from -0.21875 to 0.21875
- down_weight: bfloat16 [3072, 768], P(('dp', 'ctx')), may hold values from -0.109375 to 0.109375
- vectors: bfloat16 [8, 768], P(None, ('dp', 'ctx')), may hold values from -2 to 2
- up_bias: bfloat16 [3072], P(('dp', 'ctx')), may hold values from -4 to 4
- cotangent: bfloat16 [48, 1024, 768], P('dp', 'ctx'), may hold values from -6 to 6
Outputs:
- block_out: bfloat16 [48, 1024, 768], P('dp', 'ctx')
- input_grad: float32 [48, 1024, 768], P('dp', 'ctx')
- qkv_grad: float32 [768, 2304], P(('dp', 'ctx'))
- out_grad: float32 [768, 768], P(('dp', 'ctx'))
- up_grad: float32 [768, 3072], P(('dp', 'ctx'))
- down_grad: float32 [3072, 768], P(('dp', 'ctx'))
- vector_grad: float32 [8, 768], P(None, ('dp', 'ctx'))
- up_bias_grad: float32 [3072], P(('dp', 'ctx'))
The draws below stay inside these ranges and needn't reach their ends.
Inputs may be any that keep to these rules, and one draw needn't show every extreme that they name: segments never fall along a sequence, start at 0 and end at 3.
All inputs are finite; a program needn't handle non-finite values.
Results may differ from the reference program's by a relative error of at most 0.01.
Values may be sent and summed in bfloat16 or wider, within the bound.
A program may use at most 320 MiB of HBM per device.

```python
import jax
import jax.numpy as jnp
from jax import lax

D = 768
HEADS = 12
FF = 3072
MB = 3
CUTS = 3
SEQLEN = 1024
SPAN = 512
SEQS = 48


def draw_segments(key, part):
    key = jax.random.fold_in(key, 7)
    subkeys = jax.random.split(key, 5)
    groups = SEQS // MB
    boundary = jax.random.randint(subkeys[0], (SEQS, CUTS), 1, SEQLEN)
    chosen = jax.random.randint(subkeys[1], (groups,), 0, MB)
    flagged = jnp.arange(SEQS) % MB == jnp.repeat(chosen, MB)
    upper_side = jax.random.randint(subkeys[2], (SEQS, CUTS), 0, 2)
    early_cut = jax.random.randint(subkeys[3], (SEQS, CUTS), 1, SPAN)
    late_cut = jax.random.randint(subkeys[4], (SEQS, CUTS), SEQLEN - SPAN + 1, SEQLEN)
    edge_cut = jnp.where(upper_side == 1, late_cut, early_cut)
    boundary = jnp.where(flagged[:, None], edge_cut, boundary)
    position = jnp.arange(SEQLEN, dtype=jnp.int32)
    return jnp.sum((boundary[:, None, :] <= position[None, :, None]).astype(jnp.int32), axis=-1)


def draw_vectors(key, part):
    key = jax.random.fold_in(key, 11)
    sample = jnp.clip(jax.random.normal(key, (8, D), jnp.float32), -4.0, 4.0)
    spread = jnp.array([0.25, 0.3, 0.5, 0.3, 0.3, 0.25, 0.3, 0.3], jnp.float32)
    centre = jnp.array([1.0, 0.0, 0.0, 0.0, 0.0, 1.0, 0.0, 0.0], jnp.float32)
    return (centre[:, None] + spread[:, None] * sample).astype(jnp.bfloat16)


def block_levels(own_key, shape, shards, low, largest):
    factor_of = 1.0
    for dim, parts in shards:
        heights = jax.random.uniform(jax.random.fold_in(jax.random.fold_in(own_key, 6), dim), (parts,), jnp.float32, low / len(shards), largest / len(shards))
        factor_of = factor_of * jnp.repeat(jnp.exp(heights), shape[dim] // parts).reshape((-1,) + (1,) * (len(shape) - 1 - dim))
    return factor_of


def noise(key, shape, scale, most, shards=(), kind=jnp.bfloat16):
    drawn = scale * jax.random.normal(key, shape, jnp.float32)
    if shards:
        drawn = drawn * block_levels(key, shape, shards, -0.22, 0.18)
    return jnp.clip(drawn, -most, most).astype(kind)


def setup_inputs(seed: int = 0) -> dict:
    streams_of = jax.random.split(jax.random.key(seed), 10)
    tokens = noise(streams_of[0], (SEQS, SEQLEN, D), 1.0, 6.0, ((0, 16), (1, 2)))
    segments = draw_segments(jax.random.fold_in(streams_of[9], 71), 0)
    qkv_weight = noise(streams_of[2], (D, 3 * D), D ** -0.5, 0.21875, ((0, 32),))
    out_weight = noise(streams_of[3], (D, D), (D // 64) ** -0.5, 1.75, ((0, 32),))
    up_weight = noise(streams_of[4], (D, FF), D ** -0.5, 0.21875, ((0, 32),))
    down_weight = noise(streams_of[5], (FF, D), FF ** -0.5, 0.109375, ((0, 32),))
    vectors = draw_vectors(jax.random.fold_in(streams_of[9], 71), 0)
    up_bias = noise(streams_of[7], (FF,), 0.3, 4.0, ((0, 32),))
    cotangent = noise(streams_of[8], (SEQS, SEQLEN, D), 1.0, 6.0, ((0, 16), (1, 2)))
    return dict(tokens=tokens, segments=segments, qkv_weight=qkv_weight, out_weight=out_weight, up_weight=up_weight, down_weight=down_weight, vectors=vectors, up_bias=up_bias, cotangent=cotangent)


EPSILON = 1e-05

@jax.custom_vjp
def low(v):
    return lax.optimization_barrier(v.astype(jnp.bfloat16)).astype(jnp.float32)

@jax.custom_vjp
def low_back(v):
    return v

def low_keep(v):
    return (low(v), None)

def low_pass(kept, grad):
    return (grad,)

def back_keep(v):
    return (v, None)

def back_low(kept, grad):
    return (low(grad),)
low.defvjp(low_keep, low_pass)
low_back.defvjp(back_keep, back_low)

def layer_norm(values, norm_gain, norm_shift):
    average = lax.optimization_barrier(jnp.mean(values, -1, keepdims=True))
    centred = values - average
    variance = lax.optimization_barrier(jnp.mean(centred * centred, -1, keepdims=True))
    return centred * lax.rsqrt(variance + EPSILON) * norm_gain + norm_shift

def one_sequence(seq_rows, seq_segments, qkv_weight, out_weight, up_weight, down_weight, vectors, up_bias):
    highest = lax.Precision.HIGHEST
    seq_length, model_width = seq_rows.shape
    head_dim = model_width // HEADS
    hidden = low(layer_norm(seq_rows, vectors[0], vectors[1]))
    mixed = jnp.dot(hidden, qkv_weight, precision=highest)
    query = low(low_back(mixed[:, :model_width] + vectors[2])).reshape(seq_length, HEADS, head_dim)
    keyed = low(low_back(mixed[:, model_width:2 * model_width])).reshape(seq_length, HEADS, head_dim)
    valued = low(low_back(mixed[:, 2 * model_width:] + vectors[3])).reshape(seq_length, HEADS, head_dim)
    position = jnp.arange(seq_length, dtype=jnp.int32)
    allowed = (position[None, :] <= position[:, None]) & (seq_segments[None, :] == seq_segments[:, None])
    scores = jnp.einsum('qhd,khd->hqk', query, keyed, precision=highest) * head_dim ** (-0.5)
    scores = low_back(jnp.where(allowed[None], scores, -1e+30))
    probs = low(jax.nn.softmax(scores, axis=-1))
    attended = jnp.einsum('hqk,khd->qhd', probs, valued, precision=highest).reshape(seq_length, model_width)
    attended = low(low_back(attended))
    branch = low_back(jnp.dot(attended, out_weight, precision=highest) + vectors[4])
    middle = seq_rows + branch
    inner = low(layer_norm(middle, vectors[5], vectors[6]))
    pre_act = low_back(jnp.dot(inner, up_weight, precision=highest) + up_bias)
    active = low(jax.nn.gelu(pre_act, approximate=True))
    return middle + low_back(jnp.dot(active, down_weight, precision=highest) + vectors[7])

def reference(tokens, segments, qkv_weight, out_weight, up_weight, down_weight, vectors, up_bias, cotangent):
    floats = tuple((array.astype(jnp.float32) for array in (tokens, qkv_weight, out_weight, up_weight, down_weight, vectors, up_bias)))

    def forward(all_rows, w_qkv, w_out, w_up, w_down, vec_all, bias_all):
        checked = jax.checkpoint(one_sequence)

        def step(carry, item):
            return (carry, checked(item[0], item[1], w_qkv, w_out, w_up, w_down, vec_all, bias_all))
        unused, result = lax.scan(step, jnp.zeros((), jnp.float32), (all_rows, segments))
        return result
    result, pull_back = jax.vjp(forward, *floats)
    grads = pull_back(cotangent.astype(jnp.float32))
    return (result.astype(jnp.bfloat16), grads[0], grads[1], grads[2], grads[3], grads[4], grads[5], grads[6])
```

```python
import functools

import jax
import jax.numpy as jnp
from jax import lax
from jax.experimental import pallas as pl
from jax.experimental.pallas import tpu as pltpu
from jax.sharding import PartitionSpec as P

HEADS = 12
EPSILON = 1e-05
LANES = 128
BLOCK = 256
MASKED = -1e30
F32 = jnp.float32
BF16 = jnp.bfloat16


def layer_norm(values, norm_gain, norm_shift):
    average = jnp.mean(values, -1, keepdims=True)
    centred = values - average
    variance = jnp.mean(centred * centred, -1, keepdims=True)
    return centred * lax.rsqrt(variance + EPSILON) * norm_gain + norm_shift


def gelu_tanh(pre_act):
    return jax.nn.gelu(pre_act, approximate=True)


def dot(left, right):
    return jnp.dot(left, right, preferred_element_type=F32)


def contract_rows(left, right):
    return lax.dot_general(left, right, (((0,), (0,)), ((), ())), preferred_element_type=F32)


def contract_cols(left, right):
    return lax.dot_general(left, right, (((1,), (1,)), ((), ())), preferred_element_type=F32)


def split_pair(pair, left_lanes):
    zero = jnp.zeros_like(pair)
    return jnp.where(left_lanes, pair, zero), jnp.where(left_lanes, zero, pair)


def fill_bias(place_ref, q_seg_ref, k_seg_ref, bias_ref):
    rows = q_seg_ref.shape[0]
    for block in range(bias_ref.shape[0]):
        row = lax.broadcasted_iota(jnp.int32, (rows, BLOCK), 0) + place_ref[0]
        col = lax.broadcasted_iota(jnp.int32, (rows, BLOCK), 1) + block * BLOCK
        same = q_seg_ref[...] == k_seg_ref[:, block * BLOCK : (block + 1) * BLOCK]
        bias_ref[block] = jnp.where((col <= row) & same, 0.0, MASKED)


def attend_kernel(
    factor, first_ref, place_ref, q_ref, k_ref, v_ref, q_seg_ref, k_seg_ref, o_ref, lse_ref, bias_ref
):
    @pl.when(pl.program_id(0) == 0)
    def _():
        fill_bias(place_ref, q_seg_ref, k_seg_ref, bias_ref)

    left_lanes = lax.broadcasted_iota(jnp.int32, (BLOCK, LANES), 1) < LANES // 2
    for q_block in range(q_ref.shape[0] // BLOCK):
        span = slice(q_block * BLOCK, (q_block + 1) * BLOCK)
        queries = split_pair((q_ref[span, :] * factor).astype(BF16), left_lanes)

        def step(block, carry):
            place = pl.ds(pl.multiple_of(block * BLOCK, BLOCK), BLOCK)
            keys, values = k_ref[place, :], v_ref[place, :]
            bias = bias_ref[block, span, :]
            after = []
            for query, (top, total, summed) in zip(queries, carry):
                scores = contract_cols(query, keys) + bias
                new_top = jnp.maximum(top, jnp.max(scores, -1, keepdims=True))
                expo = jnp.exp(scores - new_top)
                shrink = jnp.exp(top - new_top)
                total = total * shrink + jnp.sum(expo, -1, keepdims=True)
                summed = summed * shrink + dot(expo.astype(BF16), values)
                after.append((new_top, total, summed))
            return tuple(after)

        begin = (
            jnp.full((BLOCK, 1), MASKED, F32),
            jnp.zeros((BLOCK, 1), F32),
            jnp.zeros((BLOCK, LANES), F32),
        )
        last = place_ref[0] // BLOCK + q_block + 1
        (top_a, total_a, sum_a), (top_b, total_b, sum_b) = lax.fori_loop(
            first_ref[q_block], last, step, (begin, begin)
        )
        o_ref[span, :] = jnp.where(left_lanes, sum_a / total_a, sum_b / total_b).astype(BF16)
        lse_ref[span, :] = jnp.where(
            left_lanes, top_a + jnp.log(total_a), top_b + jnp.log(total_b)
        )


def attend_back_kernel(
    factor,
    first_ref,
    place_ref,
    q_ref,
    k_ref,
    v_ref,
    q_seg_ref,
    k_seg_ref,
    o_ref,
    lse_ref,
    do_ref,
    dq_ref,
    dk_ref,
    dv_ref,
    bias_ref,
    dk_sum,
    dv_sum,
):
    @pl.when(pl.program_id(0) == 0)
    def _():
        fill_bias(place_ref, q_seg_ref, k_seg_ref, bias_ref)

    dk_sum[...] = jnp.zeros_like(dk_sum)
    dv_sum[...] = jnp.zeros_like(dv_sum)
    left_lanes = lax.broadcasted_iota(jnp.int32, (BLOCK, LANES), 1) < LANES // 2
    for q_block in range(q_ref.shape[0] // BLOCK):
        span = slice(q_block * BLOCK, (q_block + 1) * BLOCK)
        queries = split_pair((q_ref[span, :] * factor).astype(BF16), left_lanes)
        grads = split_pair(do_ref[span, :], left_lanes)
        products = do_ref[span, :].astype(F32) * o_ref[span, :].astype(F32)
        deltas = [jnp.sum(part, -1, keepdims=True) for part in split_pair(products, left_lanes)]
        tops = (lse_ref[span, 0:1], lse_ref[span, LANES // 2 : LANES // 2 + 1])

        def step(block, grad_query):
            place = pl.ds(pl.multiple_of(block * BLOCK, BLOCK), BLOCK)
            keys, values = k_ref[place, :], v_ref[place, :]
            bias = bias_ref[block, span, :]
            grad_key = dk_sum[place, :]
            grad_value = dv_sum[place, :]
            for query, grad, delta, top, key_half in zip(
                queries, grads, deltas, tops, split_pair(keys, left_lanes)
            ):
                probs = jnp.exp(contract_cols(query, keys) + bias - top)
                grad_score = (probs * (contract_cols(grad, values) - delta)).astype(BF16)
                grad_value = grad_value + contract_rows(probs.astype(BF16), grad)
                grad_key = grad_key + contract_rows(grad_score, query)
                grad_query = grad_query + dot(grad_score, key_half)
            dk_sum[place, :] = grad_key
            dv_sum[place, :] = grad_value
            return grad_query

        last = place_ref[0] // BLOCK + q_block + 1
        grad_query = lax.fori_loop(
            first_ref[q_block], last, step, jnp.zeros((BLOCK, LANES), F32)
        )
        dq_ref[span, :] = (grad_query * factor).astype(BF16)
    dk_ref[...] = dk_sum[...].astype(BF16)
    dv_ref[...] = dv_sum[...].astype(BF16)


def attention_call(kernel, name, first, place, operands, out_types, sums, products):
    query, keys = operands[0], operands[1]
    rows, model_width = query.shape
    length = keys.shape[0]

    def spec(array):
        if array.shape[1] == model_width:
            return pl.BlockSpec((array.shape[0], LANES), lambda pair, *_: (0, pair))
        return pl.BlockSpec(array.shape, lambda pair, *_: (0, 0))

    scratch = [pltpu.VMEM((length // BLOCK, rows, BLOCK), F32)]
    scratch += [pltpu.VMEM((length, LANES), F32)] * sums
    return pl.pallas_call(
        kernel,
        grid_spec=pltpu.PrefetchScalarGridSpec(
            num_scalar_prefetch=2,
            grid=(model_width // LANES,),
            in_specs=[spec(array) for array in operands],
            out_specs=[spec(array) for array in out_types],
            scratch_shapes=scratch,
        ),
        out_shape=out_types,
        name=name,
        compiler_params=pltpu.CompilerParams(vmem_limit_bytes=40 * 1024 * 1024),
        cost_estimate=pl.CostEstimate(
            flops=products * 8 * rows * length * model_width,
            bytes_accessed=16 * length * model_width,
            transcendentals=HEADS * rows * length,
        ),
    )(first, place, *operands)


def on_device(
    tokens, segments, qkv_weight, out_weight, up_weight, down_weight, vectors, up_bias, cotangent
):
    micro_count, span_rows, width = tokens.shape
    head_dim = width // HEADS
    factor = head_dim ** (-0.5)
    row_share = qkv_weight.shape[0]
    both = ("dp", "ctx")
    ctx_size = lax.axis_size("ctx")
    ctx_place = lax.axis_index("ctx")
    q_start = ctx_place * span_rows
    neighbours = ctx_size == 2

    def gather(shard):
        return lax.all_gather(shard, both, axis=0, tiled=True)

    def scatter(whole):
        return lax.psum_scatter(whole.astype(BF16), both, scatter_dimension=0, tiled=True)

    vec_count = vectors.shape[0]
    bias_count = up_bias.shape[0] // row_share
    extra_count = vec_count + bias_count
    extra = jnp.concatenate([vectors.T, up_bias.reshape(row_share, bias_count)], 1)
    extra = jnp.pad(extra, ((0, 0), (0, LANES - extra_count)))
    wide = gather(jnp.concatenate([qkv_weight, extra], 1))
    w_out = gather(out_weight)
    w_up = gather(up_weight)
    w_down = gather(down_weight)
    w_qkv = wide[:, : 3 * width]
    small = wide[:, 3 * width : 3 * width + extra_count].astype(F32)
    vec_rows = small[:, :vec_count].T
    bias_all = small[:, vec_count:].reshape(-1)

    token_rows = tokens.reshape(micro_count * span_rows, width).astype(F32)
    hidden = layer_norm(token_rows, vec_rows[0], vec_rows[1]).astype(BF16)
    mixed_kv = dot(hidden, w_qkv[:, width:])
    key_value = jnp.concatenate(
        [mixed_kv[:, :width].astype(BF16), (mixed_kv[:, width:] + vec_rows[3]).astype(BF16)], 1
    ).reshape(micro_count, span_rows, 2 * width)
    query_all = (dot(hidden, w_qkv[:, :width]) + vec_rows[2]).astype(BF16)
    query_all = query_all.reshape(micro_count, span_rows, width)

    saved = []
    attended = []
    for micro in range(micro_count):
        own_kv = key_value[micro]
        seq_segs = segments[micro]
        own_segs = lax.dynamic_slice_in_dim(seq_segs, q_start, span_rows)
        if neighbours:
            before = lax.ppermute(own_kv, "ctx", [(0, 1)])
            all_kv = jnp.concatenate([before, own_kv], 0)
            k_segs = jnp.concatenate(
                [jnp.where(ctx_place == 0, -1, seq_segs[:span_rows]), own_segs], 0
            )
            place = jnp.full((1,), span_rows, jnp.int32)
        else:
            all_kv = lax.all_gather(own_kv, "ctx", axis=0, tiled=True)
            k_segs = seq_segs
            place = jnp.full((1,), q_start, jnp.int32)
        starts = own_segs[::BLOCK]
        first = jnp.sum((k_segs[None, :] < starts[:, None]).astype(jnp.int32), 1) // BLOCK
        operands = (
            query_all[micro],
            all_kv[:, :width],
            all_kv[:, width:],
            own_segs[:, None],
            k_segs[None, :],
        )
        low_rows = jax.ShapeDtypeStruct((span_rows, width), BF16)
        out, lse = attention_call(
            functools.partial(attend_kernel, factor),
            "attend",
            first,
            place,
            operands,
            [low_rows, jax.ShapeDtypeStruct((span_rows, width), F32)],
            0,
            1,
        )
        saved.append((first, place, operands, out, lse))
        attended.append(out)
    attended = jnp.concatenate(attended, 0)

    middle = token_rows + dot(attended, w_out) + vec_rows[4]
    inner = layer_norm(middle, vec_rows[5], vec_rows[6]).astype(BF16)
    pre_act = dot(inner, w_up) + bias_all
    active = gelu_tanh(pre_act).astype(BF16)
    result = (middle + dot(active, w_down) + vec_rows[7]).astype(BF16)

    grad_low = cotangent.reshape(micro_count * span_rows, width)
    grad_rows = grad_low.astype(F32)
    own_down = scatter(contract_rows(active, grad_low))
    grad_bdown = jnp.sum(grad_rows, 0)
    grad_act = contract_cols(grad_low, w_down)
    grad_pre = jax.vjp(gelu_tanh, pre_act)[1](grad_act)[0].astype(BF16)
    own_up = scatter(contract_rows(inner, grad_pre))
    grad_bias = jnp.sum(grad_pre.astype(F32), 0)
    grad_inner = contract_cols(grad_pre, w_up)
    norm_two_back = jax.vjp(layer_norm, middle, vec_rows[5], vec_rows[6])[1]
    grad_mid_norm, grad_gain_two, grad_shift_two = norm_two_back(grad_inner)
    grad_middle = grad_rows + grad_mid_norm
    grad_branch = grad_middle.astype(BF16)
    own_out = scatter(contract_rows(attended, grad_branch))
    grad_bout = jnp.sum(grad_branch.astype(F32), 0)
    grad_att = contract_cols(grad_branch, w_out).astype(BF16)
    grad_att = grad_att.reshape(micro_count, span_rows, width)

    grad_queries = []
    grad_kvs = []
    for micro in range(micro_count):
        first, place, operands, out, lse = saved[micro]
        low_keys = jax.ShapeDtypeStruct(operands[1].shape, BF16)
        grad_query, grad_key, grad_value = attention_call(
            functools.partial(attend_back_kernel, factor),
            "attend_back",
            first,
            place,
            operands + (out, lse, grad_att[micro]),
            [jax.ShapeDtypeStruct((span_rows, width), BF16), low_keys, low_keys],
            2,
            3,
        )
        grad_queries.append(grad_query)
        kv_terms = jnp.concatenate([grad_key, grad_value], 1)
        if neighbours:
            theirs = lax.ppermute(kv_terms[:span_rows], "ctx", [(1, 0)])
            own = kv_terms[span_rows:].astype(F32) + theirs.astype(F32)
        else:
            own = lax.psum_scatter(kv_terms, "ctx", scatter_dimension=0, tiled=True)
        grad_kvs.append(own.astype(BF16))
    grad_query = jnp.concatenate(grad_queries, 0)
    grad_kv = jnp.concatenate(grad_kvs, 0)
    grad_mixed = jnp.concatenate([grad_query, grad_kv], 1)
    grad_qkv = contract_rows(hidden, grad_mixed)
    column_sums = jnp.sum(grad_mixed.astype(F32), 0)
    grad_hidden = contract_cols(grad_mixed, w_qkv)
    norm_one_back = jax.vjp(layer_norm, token_rows, vec_rows[0], vec_rows[1])[1]
    grad_tok_norm, grad_gain_one, grad_shift_one = norm_one_back(grad_hidden)
    input_grad = grad_middle + grad_tok_norm
    grad_vec = jnp.stack(
        [
            grad_gain_one,
            grad_shift_one,
            column_sums[:width],
            column_sums[2 * width :],
            grad_bout,
            grad_gain_two,
            grad_shift_two,
            grad_bdown,
        ]
    )
    grad_extra = jnp.concatenate([grad_vec.T, grad_bias.reshape(width, bias_count)], 1)
    grad_extra = jnp.pad(grad_extra, ((0, 0), (0, LANES - extra_count)))
    own_wide = scatter(jnp.concatenate([grad_qkv, grad_extra], 1)).astype(F32)
    own_small = own_wide[:, 3 * width : 3 * width + extra_count]
    return (
        result.reshape(tokens.shape),
        input_grad.reshape(tokens.shape),
        own_wide[:, : 3 * width],
        own_out.astype(F32),
        own_up.astype(F32),
        own_down.astype(F32),
        own_small[:, :vec_count].T,
        own_small[:, vec_count:].reshape(-1),
    )


def solution(mesh):
    rows = P(("dp", "ctx"), None)
    spans = P("dp", "ctx", None)
    tail = (rows, rows, rows, rows, P(None, ("dp", "ctx")), P(("dp", "ctx")))
    return jax.shard_map(
        on_device,
        mesh=mesh,
        in_specs=(spans, P("dp", None)) + tail + (spans,),
        out_specs=(spans, spans) + tail,
        check_vma=False,
    )
```

```python
import functools

import jax
import jax.numpy as jnp
from jax import lax
from jax.experimental import pallas as pl
from jax.experimental.pallas import tpu as pltpu
from jax.sharding import PartitionSpec as P

HEADS = 12
EPSILON = 1e-05
LANES = 128
BLOCK = 256
MASKED = -1e30
F32 = jnp.float32
BF16 = jnp.bfloat16


def layer_norm(values, norm_gain, norm_shift):
    average = jnp.mean(values, -1, keepdims=True)
    centred = values - average
    variance = jnp.mean(centred * centred, -1, keepdims=True)
    return centred * lax.rsqrt(variance + EPSILON) * norm_gain + norm_shift


def gelu_tanh(pre_act):
    return jax.nn.gelu(pre_act, approximate=True)


def dot(left, right):
    return jnp.dot(left, right, preferred_element_type=F32)


def contract_rows(left, right):
    return lax.dot_general(left, right, (((0,), (0,)), ((), ())), preferred_element_type=F32)


def contract_cols(left, right):
    return lax.dot_general(left, right, (((1,), (1,)), ((), ())), preferred_element_type=F32)


def split_pair(pair, left_lanes):
    zero = jnp.zeros_like(pair)
    return jnp.where(left_lanes, pair, zero), jnp.where(left_lanes, zero, pair)


def fill_bias(place_ref, q_seg_ref, k_seg_ref, bias_ref):
    rows = q_seg_ref.shape[0]
    for block in range(bias_ref.shape[0]):
        row = lax.broadcasted_iota(jnp.int32, (rows, BLOCK), 0) + place_ref[0]
        col = lax.broadcasted_iota(jnp.int32, (rows, BLOCK), 1) + block * BLOCK
        same = q_seg_ref[...] == k_seg_ref[:, block * BLOCK : (block + 1) * BLOCK]
        bias_ref[block] = jnp.where((col <= row) & same, 0.0, MASKED)


def attend_kernel(
    factor, first_ref, place_ref, q_ref, k_ref, v_ref, q_seg_ref, k_seg_ref, o_ref, lse_ref, bias_ref
):
    @pl.when(pl.program_id(0) == 0)
    def _():
        fill_bias(place_ref, q_seg_ref, k_seg_ref, bias_ref)

    left_lanes = lax.broadcasted_iota(jnp.int32, (BLOCK, LANES), 1) < LANES // 2
    for q_block in range(q_ref.shape[0] // BLOCK):
        span = slice(q_block * BLOCK, (q_block + 1) * BLOCK)
        queries = split_pair((q_ref[span, :] * factor).astype(BF16), left_lanes)

        def step(block, carry):
            place = pl.ds(pl.multiple_of(block * BLOCK, BLOCK), BLOCK)
            keys, values = k_ref[place, :], v_ref[place, :]
            bias = bias_ref[block, span, :]
            after = []
            for query, (top, total, summed) in zip(queries, carry):
                scores = contract_cols(query, keys) + bias
                new_top = jnp.maximum(top, jnp.max(scores, -1, keepdims=True))
                expo = jnp.exp(scores - new_top)
                shrink = jnp.exp(top - new_top)
                total = total * shrink + jnp.sum(expo, -1, keepdims=True)
                summed = summed * shrink + dot(expo.astype(BF16), values)
                after.append((new_top, total, summed))
            return tuple(after)

        begin = (
            jnp.full((BLOCK, 1), MASKED, F32),
            jnp.zeros((BLOCK, 1), F32),
            jnp.zeros((BLOCK, LANES), F32),
        )
        last = place_ref[0] // BLOCK + q_block + 1
        (top_a, total_a, sum_a), (top_b, total_b, sum_b) = lax.fori_loop(
            first_ref[q_block], last, step, (begin, begin)
        )
        o_ref[span, :] = jnp.where(left_lanes, sum_a / total_a, sum_b / total_b).astype(BF16)
        lse_ref[span, :] = jnp.where(
            left_lanes, top_a + jnp.log(total_a), top_b + jnp.log(total_b)
        )


def attend_back_kernel(
    factor,
    first_ref,
    place_ref,
    q_ref,
    k_ref,
    v_ref,
    q_seg_ref,
    k_seg_ref,
    o_ref,
    lse_ref,
    do_ref,
    dq_ref,
    dk_ref,
    dv_ref,
    bias_ref,
    dk_sum,
    dv_sum,
):
    @pl.when(pl.program_id(0) == 0)
    def _():
        fill_bias(place_ref, q_seg_ref, k_seg_ref, bias_ref)

    dk_sum[...] = jnp.zeros_like(dk_sum)
    dv_sum[...] = jnp.zeros_like(dv_sum)
    left_lanes = lax.broadcasted_iota(jnp.int32, (BLOCK, LANES), 1) < LANES // 2
    for q_block in range(q_ref.shape[0] // BLOCK):
        span = slice(q_block * BLOCK, (q_block + 1) * BLOCK)
        queries = split_pair((q_ref[span, :] * factor).astype(BF16), left_lanes)
        grads = split_pair(do_ref[span, :], left_lanes)
        products = do_ref[span, :].astype(F32) * o_ref[span, :].astype(F32)
        deltas = [jnp.sum(part, -1, keepdims=True) for part in split_pair(products, left_lanes)]
        tops = (lse_ref[span, 0:1], lse_ref[span, LANES // 2 : LANES // 2 + 1])

        def step(block, grad_query):
            place = pl.ds(pl.multiple_of(block * BLOCK, BLOCK), BLOCK)
            keys, values = k_ref[place, :], v_ref[place, :]
            bias = bias_ref[block, span, :]
            grad_key = dk_sum[place, :]
            grad_value = dv_sum[place, :]
            for query, grad, delta, top, key_half in zip(
                queries, grads, deltas, tops, split_pair(keys, left_lanes)
            ):
                probs = jnp.exp(contract_cols(query, keys) + bias - top)
                grad_score = (probs * (contract_cols(grad, values) - delta)).astype(BF16)
                grad_value = grad_value + contract_rows(probs.astype(BF16), grad)
                grad_key = grad_key + contract_rows(grad_score, query)
                grad_query = grad_query + dot(grad_score, key_half)
            dk_sum[place, :] = grad_key
            dv_sum[place, :] = grad_value
            return grad_query

        last = place_ref[0] // BLOCK + q_block + 1
        grad_query = lax.fori_loop(
            first_ref[q_block], last, step, jnp.zeros((BLOCK, LANES), F32)
        )
        dq_ref[span, :] = (grad_query * factor).astype(BF16)
    dk_ref[...] = dk_sum[...].astype(BF16)
    dv_ref[...] = dv_sum[...].astype(BF16)


def attention_call(kernel, name, first, place, operands, out_types, sums, products):
    query, keys = operands[0], operands[1]
    rows, model_width = query.shape
    length = keys.shape[0]

    def spec(array):
        if array.shape[1] == model_width:
            return pl.BlockSpec((array.shape[0], LANES), lambda pair, *_: (0, pair))
        return pl.BlockSpec(array.shape, lambda pair, *_: (0, 0))

    scratch = [pltpu.VMEM((length // BLOCK, rows, BLOCK), F32)]
    scratch += [pltpu.VMEM((length, LANES), F32)] * sums
    return pl.pallas_call(
        kernel,
        grid_spec=pltpu.PrefetchScalarGridSpec(
            num_scalar_prefetch=2,
            grid=(model_width // LANES,),
            in_specs=[spec(array) for array in operands],
            out_specs=[spec(array) for array in out_types],
            scratch_shapes=scratch,
        ),
        out_shape=out_types,
        name=name,
        compiler_params=pltpu.CompilerParams(vmem_limit_bytes=40 * 1024 * 1024),
        cost_estimate=pl.CostEstimate(
            flops=products * 8 * rows * length * model_width,
            bytes_accessed=16 * length * model_width,
            transcendentals=HEADS * rows * length,
        ),
    )(first, place, *operands)


def on_device(
    tokens, segments, qkv_weight, out_weight, up_weight, down_weight, vectors, up_bias, cotangent
):
    micro_count, span_rows, width = tokens.shape
    head_dim = width // HEADS
    factor = head_dim ** (-0.5)
    row_share = qkv_weight.shape[0]
    both = ("dp", "ctx")
    ctx_size = lax.axis_size("ctx")
    ctx_place = lax.axis_index("ctx")
    q_start = ctx_place * span_rows
    neighbours = ctx_size == 2

    def gather(shard):
        return lax.all_gather(shard, both, axis=0, tiled=True)

    def scatter(whole):
        return lax.psum_scatter(whole.astype(BF16), both, scatter_dimension=0, tiled=True)

    vec_count = vectors.shape[0]
    bias_count = up_bias.shape[0] // row_share
    extra_count = vec_count + bias_count
    extra = jnp.concatenate([vectors.T, up_bias.reshape(row_share, bias_count)], 1)
    extra = jnp.pad(extra, ((0, 0), (0, LANES - extra_count)))
    wide = gather(jnp.concatenate([qkv_weight, extra], 1))
    units = up_weight.shape[1]
    rest = gather(
        jnp.concatenate([out_weight, up_weight, down_weight.reshape(row_share, units)], 1)
    )
    w_out = rest[:, :width]
    w_up = rest[:, width : width + units]
    w_down = rest[:, width + units :].reshape(units, width)
    w_qkv = wide[:, : 3 * width]
    small = wide[:, 3 * width : 3 * width + extra_count].astype(F32)
    vec_rows = small[:, :vec_count].T
    bias_all = small[:, vec_count:].reshape(-1)

    token_rows = tokens.reshape(micro_count * span_rows, width).astype(F32)
    hidden = layer_norm(token_rows, vec_rows[0], vec_rows[1]).astype(BF16)
    mixed_kv = dot(hidden, w_qkv[:, width:])
    key_value = jnp.concatenate(
        [mixed_kv[:, :width].astype(BF16), (mixed_kv[:, width:] + vec_rows[3]).astype(BF16)], 1
    ).reshape(micro_count, span_rows, 2 * width)
    query_all = (dot(hidden, w_qkv[:, :width]) + vec_rows[2]).astype(BF16)
    query_all = query_all.reshape(micro_count, span_rows, width)

    saved = []
    attended = []
    for micro in range(micro_count):
        own_kv = key_value[micro]
        seq_segs = segments[micro]
        own_segs = lax.dynamic_slice_in_dim(seq_segs, q_start, span_rows)
        if neighbours:
            before = lax.ppermute(own_kv, "ctx", [(0, 1)])
            all_kv = jnp.concatenate([before, own_kv], 0)
            k_segs = jnp.concatenate(
                [jnp.where(ctx_place == 0, -1, seq_segs[:span_rows]), own_segs], 0
            )
            place = jnp.full((1,), span_rows, jnp.int32)
        else:
            all_kv = lax.all_gather(own_kv, "ctx", axis=0, tiled=True)
            k_segs = seq_segs
            place = jnp.full((1,), q_start, jnp.int32)
        starts = own_segs[::BLOCK]
        first = jnp.sum((k_segs[None, :] < starts[:, None]).astype(jnp.int32), 1) // BLOCK
        operands = (
            query_all[micro],
            all_kv[:, :width],
            all_kv[:, width:],
            own_segs[:, None],
            k_segs[None, :],
        )
        low_rows = jax.ShapeDtypeStruct((span_rows, width), BF16)
        out, lse = attention_call(
            functools.partial(attend_kernel, factor),
            "attend",
            first,
            place,
            operands,
            [low_rows, jax.ShapeDtypeStruct((span_rows, width), F32)],
            0,
            1,
        )
        saved.append((first, place, operands, out, lse))
        attended.append(out)
    attended = jnp.concatenate(attended, 0)

    middle = token_rows + dot(attended, w_out) + vec_rows[4]
    inner = layer_norm(middle, vec_rows[5], vec_rows[6]).astype(BF16)
    pre_act = dot(inner, w_up) + bias_all
    active = gelu_tanh(pre_act).astype(BF16)
    result = (middle + dot(active, w_down) + vec_rows[7]).astype(BF16)

    grad_low = cotangent.reshape(micro_count * span_rows, width)
    grad_rows = grad_low.astype(F32)
    grad_down = contract_rows(active, grad_low).astype(BF16).reshape(width, units)
    grad_bdown = jnp.sum(grad_rows, 0)
    grad_act = contract_cols(grad_low, w_down)
    grad_pre = jax.vjp(gelu_tanh, pre_act)[1](grad_act)[0].astype(BF16)
    grad_up = contract_rows(inner, grad_pre).astype(BF16)
    own_feed = scatter(jnp.concatenate([grad_up, grad_down], 1)).astype(F32)
    grad_bias = jnp.sum(grad_pre.astype(F32), 0)
    grad_inner = contract_cols(grad_pre, w_up)
    norm_two_back = jax.vjp(layer_norm, middle, vec_rows[5], vec_rows[6])[1]
    grad_mid_norm, grad_gain_two, grad_shift_two = norm_two_back(grad_inner)
    grad_middle = grad_rows + grad_mid_norm
    grad_branch = grad_middle.astype(BF16)
    grad_out = contract_rows(attended, grad_branch)
    grad_bout = jnp.sum(grad_branch.astype(F32), 0)
    grad_att = contract_cols(grad_branch, w_out).astype(BF16)
    grad_att = grad_att.reshape(micro_count, span_rows, width)

    grad_queries = []
    grad_kvs = []
    for micro in range(micro_count):
        first, place, operands, out, lse = saved[micro]
        low_keys = jax.ShapeDtypeStruct(operands[1].shape, BF16)
        grad_query, grad_key, grad_value = attention_call(
            functools.partial(attend_back_kernel, factor),
            "attend_back",
            first,
            place,
            operands + (out, lse, grad_att[micro]),
            [jax.ShapeDtypeStruct((span_rows, width), BF16), low_keys, low_keys],
            2,
            3,
        )
        grad_queries.append(grad_query)
        kv_terms = jnp.concatenate([grad_key, grad_value], 1)
        if neighbours:
            theirs = lax.ppermute(kv_terms[:span_rows], "ctx", [(1, 0)])
            own = kv_terms[span_rows:].astype(F32) + theirs.astype(F32)
        else:
            own = lax.psum_scatter(kv_terms, "ctx", scatter_dimension=0, tiled=True)
        grad_kvs.append(own.astype(BF16))
    grad_query = jnp.concatenate(grad_queries, 0)
    grad_kv = jnp.concatenate(grad_kvs, 0)
    grad_mixed = jnp.concatenate([grad_query, grad_kv], 1)
    grad_qkv = contract_rows(hidden, grad_mixed)
    column_sums = dot(jnp.ones((8, grad_mixed.shape[0]), BF16), grad_mixed)[0]
    grad_hidden = contract_cols(grad_mixed, w_qkv)
    norm_one_back = jax.vjp(layer_norm, token_rows, vec_rows[0], vec_rows[1])[1]
    grad_tok_norm, grad_gain_one, grad_shift_one = norm_one_back(grad_hidden)
    input_grad = grad_middle + grad_tok_norm
    grad_vec = jnp.stack(
        [
            grad_gain_one,
            grad_shift_one,
            column_sums[:width],
            column_sums[2 * width :],
            grad_bout,
            grad_gain_two,
            grad_shift_two,
            grad_bdown,
        ]
    )
    grad_extra = jnp.concatenate([grad_vec.T, grad_bias.reshape(width, bias_count)], 1)
    grad_extra = jnp.pad(grad_extra, ((0, 0), (0, LANES - extra_count)))
    own_wide = scatter(jnp.concatenate([grad_qkv, grad_out, grad_extra], 1)).astype(F32)
    own_small = own_wide[:, 4 * width : 4 * width + extra_count]
    return (
        result.reshape(tokens.shape),
        input_grad.reshape(tokens.shape),
        own_wide[:, : 3 * width],
        own_wide[:, 3 * width : 4 * width],
        own_feed[:, :units],
        own_feed[:, units:].reshape(down_weight.shape),
        own_small[:, :vec_count].T,
        own_small[:, vec_count:].reshape(-1),
    )


def solution(mesh):
    rows = P(("dp", "ctx"), None)
    spans = P("dp", "ctx", None)
    tail = (rows, rows, rows, rows, P(None, ("dp", "ctx")), P(("dp", "ctx")))
    return jax.shard_map(
        on_device,
        mesh=mesh,
        in_specs=(spans, P("dp", None)) + tail + (spans,),
        out_specs=(spans, spans) + tail,
        check_vma=False,
    )
```
